1024 devices in a mesh: seq: 64 (over z, x), head: 16 (over y, core).
Axes of the slice: x: 4, y: 8, z: 16, core: 2. Of those that a mesh axis runs over, the one named last changes fastest.
Arguments:
- vit_query: bfloat16 [16384, 6144], P('seq', 'head'), may hold values from -2.5 to 2.5
- vit_key: bfloat16 [16384, 6144], P('seq', 'head'), may hold values from -2.5 to 2.5
- vit_value: bfloat16 [16384, 6144], P('seq', 'head'), may hold values from -20 to 20
- image_proj: bfloat16 [6144, 8192], P(None, 'head'), may hold values from -2 to 2
- image_slot: int32 [64], replicated, may hold values from 0 to 63, each once
- image_offset: int32 [64], replicated, may hold values from 0 to 256
- text_embed: bfloat16 [512, 64, 8192], P(None, 'seq', 'head'), may hold values from -36 to 36
- norm_gain: float32 [8192], P('head'), may hold values from 0.1 to 1.9
- kv_weight: bfloat16 [8192, 512], P('head'), may hold values from -0.0625 to 0.0625
Outputs:
- merged: bfloat16 [512, 64, 8192], P(None, 'seq', 'head')
- keys_values: bfloat16 [512, 64, 512], P(None, 'seq')
The draws below stay inside these ranges and needn't reach their ends.
Inputs may be any that keep to these rules, and one draw needn't show every extreme that they name: `image_slot`: each of the 64 examples holds exactly one image.
All inputs are finite; a program needn't handle non-finite values.
Results may differ from the reference program's by a relative error of at most 0.0061.
Values may be sent and summed in bfloat16 or wider, within the bound.
A program may use at most 32 MiB of HBM per device.

```python
import math
import jax
import jax.numpy as jnp
from jax import lax

D = 8192
VIT_HD = 128
KV_HD = 256
IMG_TOK = 256
TOK_DEV = 512
VIT_D = 6144
EXAMPLE_LEN = 512
IMAGES = 64
SEQ_LEN = 32768
N_SEQ = 64


def draw_vit_value(key, part):
    key = jax.random.fold_in(key, 5)
    first_key, second_key = jax.random.split(key)
    image_scale = jnp.exp(jax.random.uniform(first_key, (IMAGES, 1, 1), jnp.float32, math.log(0.5), math.log(5.0)))
    values = jnp.clip(jax.random.normal(second_key, (IMAGES, IMG_TOK, VIT_D), jnp.float32), -4.0, 4.0)
    return (values * image_scale).reshape(IMAGES * IMG_TOK, VIT_D).astype(jnp.bfloat16)


def draw_image_proj(key, part):
    key = jax.random.fold_in(key, 7)
    first_key, second_key = jax.random.split(key)
    ramp = 1.0 + jnp.arange(D, dtype=jnp.float32)[None, :] / D
    column_scale = jnp.exp(jax.random.uniform(first_key, (1, D), jnp.float32, 0.0, math.log(5.0))) * ramp * 0.5
    values = jnp.clip(jax.random.normal(second_key, (VIT_D, D), jnp.float32), -4.0, 4.0)
    return (values * column_scale / math.sqrt(VIT_D)).astype(jnp.bfloat16)


def draw_text_embed(key, part):
    key = jax.random.fold_in(key, 11)
    first_key, second_key, third_key = jax.random.split(key, 3)
    seq_width = SEQ_LEN // TOK_DEV
    row_scale = jnp.exp(jax.random.uniform(first_key, (TOK_DEV, seq_width, 1), jnp.float32, math.log(0.3), math.log(3.0)))
    ramp = 1.0 + jnp.arange(D, dtype=jnp.float32)[None, None, :] / D
    column_scale = jnp.exp(jax.random.uniform(second_key, (1, 1, D), jnp.float32, 0.0, math.log(5.0))) * ramp * 0.3
    values = jnp.clip(jax.random.normal(third_key, (TOK_DEV, seq_width, D), jnp.float32), -4.0, 4.0)
    return (values * row_scale * column_scale).astype(jnp.bfloat16)


def with_ends(entries, stream_key, least, largest):
    shape = entries.shape
    index_at = [jax.random.randint(jax.random.fold_in(stream_key, axis), (), 0, shape[axis]) for axis in range(len(shape))]
    entries = entries.at[tuple(index_at)].set(least)
    longest = shape.index(max(shape))
    index_at[longest] = (index_at[longest] + 1) % shape[longest]
    return entries.at[tuple(index_at)].set(largest)


def steps_of(rng, shape, shards, smallest, top_value):
    factor_of, own = 1.0, jax.random.fold_in(rng, 6)
    for position, blocks in shards:
        steps = jnp.exp(jax.random.uniform(jax.random.fold_in(own, position), (blocks,), jnp.float32, smallest / len(shards), top_value / len(shards)))
        factor_of = factor_of * jnp.repeat(steps, shape[position] // blocks).reshape([-1 if axis == position else 1 for axis in range(len(shape))])
    return factor_of


def bell_draw(own_key, dims, deviation, reach, pieces=(), kind=jnp.bfloat16):
    array = jax.random.normal(own_key, dims, jnp.float32) * deviation
    if len(pieces) > 0:
        array = steps_of(own_key, dims, pieces, -0.22, 0.18) * array
    return jnp.clip(array, min=-reach, max=reach).astype(kind)


def setup_inputs(seed: int = 0) -> dict:
    splits = jax.random.split(jax.random.key(seed), 10)
    return {
        "vit_query": bell_draw(splits[0], (IMAGES * IMG_TOK, VIT_D), 1.0, 2.5, ((0, 64), (1, 16))),
        "vit_key": bell_draw(splits[1], (IMAGES * IMG_TOK, VIT_D), 1.0, 2.5, ((0, 64), (1, 16))),
        "vit_value": draw_vit_value(jax.random.fold_in(splits[9], 71), 0),
        "image_proj": draw_image_proj(jax.random.fold_in(splits[9], 71), 0),
        "image_slot": jax.random.permutation(splits[4], IMAGES).astype(jnp.int32),
        "image_offset": with_ends(jax.random.randint(splits[5], (IMAGES,), 0, EXAMPLE_LEN - IMG_TOK + 1), jax.random.fold_in(splits[5], 1), 0, EXAMPLE_LEN - IMG_TOK).astype(jnp.int32),
        "text_embed": draw_text_embed(jax.random.fold_in(splits[9], 71), 0),
        "norm_gain": jnp.clip(1.0 + 0.18 * jax.random.normal(splits[7], (D,), jnp.float32), 0.1, 1.9),
        "kv_weight": bell_draw(splits[8], (D, 2 * KV_HD), D ** -0.5, 0.0625, ((0, 16),)),
    }


def rotate(key_part, positions):
    half_dim = KV_HD // 2
    exponent = jnp.arange(half_dim, dtype=jnp.float32) * (2.0 / KV_HD)
    frequency = jnp.power(jnp.float32(10000.0), -exponent)
    angles = positions.astype(jnp.float32)[:, None] * frequency[None, :]
    cosine = jnp.cos(angles)
    sine_of = jnp.sin(angles)
    first_half = key_part[:, :half_dim]
    second_half = key_part[:, half_dim:]
    return jnp.concatenate([first_half * cosine - second_half * sine_of, second_half * cosine + first_half * sine_of], axis=1)

def attend(image_query, image_key, image_value):
    scores = jnp.einsum('iahd,ibhd->ihab', image_query.astype(jnp.float32), image_key.astype(jnp.float32)) / math.sqrt(VIT_HD)
    weights = jnp.exp(scores)
    attention = (weights / lax.optimization_barrier(jnp.sum(weights, axis=-1, keepdims=True))).astype(jnp.bfloat16)
    mixed_rows = jnp.einsum('ihab,ibhd->iahd', attention.astype(jnp.float32), image_value.astype(jnp.float32))
    return mixed_rows.astype(jnp.bfloat16)

def reference(vit_query, vit_key, vit_value, image_proj, image_slot, image_offset, text_embed, norm_gain, kv_weight):
    head_count = VIT_D // VIT_HD
    shaped = (IMAGES, 1, IMG_TOK, head_count, VIT_HD)

    def encode_one(operands):
        vision_out = attend(operands[0], operands[1], operands[2]).reshape(IMG_TOK, VIT_D)
        return jnp.dot(vision_out, image_proj, preferred_element_type=jnp.float32).astype(jnp.bfloat16)
    image_tokens = lax.map(encode_one, (vit_query.reshape(shaped), vit_key.reshape(shaped), vit_value.reshape(shaped)))
    image_tokens = image_tokens.reshape(IMAGES * IMG_TOK, D)
    starts = image_slot * EXAMPLE_LEN + image_offset
    placed = (starts[:, None] + jnp.arange(IMG_TOK, dtype=jnp.int32)[None, :]).reshape(IMAGES * IMG_TOK)
    merged = text_embed.reshape(SEQ_LEN, D).at[placed].set(image_tokens)

    def layer_block(block_index):
        rows_here = lax.dynamic_slice_in_dim(merged, block_index * TOK_DEV, TOK_DEV, 0)
        positions = block_index * TOK_DEV + jnp.arange(TOK_DEV, dtype=jnp.int32)
        widened = rows_here.astype(jnp.float32)
        squares = lax.optimization_barrier(jnp.sum(widened * widened, axis=1))
        inverse = 1.0 / jnp.sqrt(squares / D + 1e-06)
        scaled = (widened * norm_gain.astype(jnp.float32)[None, :]).astype(jnp.bfloat16)
        projected = jnp.dot(scaled, kv_weight, preferred_element_type=jnp.float32) * inverse[:, None]
        rotated = rotate(projected[:, :KV_HD], positions)
        return jnp.concatenate([rotated, projected[:, KV_HD:]], axis=1).astype(jnp.bfloat16)
    blocks = lax.map(layer_block, jnp.arange(N_SEQ, dtype=jnp.int32))
    keys_values = blocks.reshape(TOK_DEV, N_SEQ, 2 * KV_HD)
    return (merged.reshape(TOK_DEV, N_SEQ, D), keys_values)
```

```python
import functools
import math

import jax
import jax.numpy as jnp
import numpy as np
from jax import lax
from jax.experimental import pallas as pl
from jax.experimental.pallas import tpu as pltpu
from jax.sharding import PartitionSpec as P

KV_HD = 256
VIT_HD = 128
HEADS = 3
FEAT = 512
KV = 512
KEEP = 4
PACK = FEAT // 128 * KEEP
SIDE = KV_HD + 128
MESH = pl.DeviceIdType.MESH
F32 = jnp.float32
BF16 = jnp.bfloat16


def log2(n):
    return n.bit_length() - 1


def dot(a, b):
    return jnp.dot(a, b, preferred_element_type=F32)


def one_hot(hits):
    return jnp.where(hits, 1.0, 0.0).astype(BF16)


def kernel(
    sizes,
    q_hbm, k_hbm, v_hbm, w_hbm, text_hbm, kvw_hbm, gain, slot_s, offset_s,
    slot_row, offset_row, slot_col, offset_col, freq,
    merged_hbm, kv_hbm,
    q_v, k_v, v_v, w_v, text_v, kvw_v, qp, att, acc, pack_m, unpack_m,
    send_b, recv_b, tok, place, pos, trig, halves, sib_b, rs_send, rs_recv, kvfin, merged_v, kv_v, kv_acc,
    load_sem, out_sem, ring_send, ring_recv, sib_send, sib_recv, a2a_send, a2a_recv,
    half_send, half_recv, rs_ssem, rs_rsem, ag_ssem, ag_rsem, fwd_send, fwd_recv,
):
    n_seq, nz, nx, ny, chunks, img_tok, example_len, d_model = sizes
    hops = ny // 2
    rc = img_tok // chunks
    nj = rc // KEEP
    local_rows = example_len * n_seq // n_seq
    per_example = example_len // n_seq
    group_rows = (img_tok, img_tok // 2, img_tok // 2)
    group_base = (0, img_tok, img_tok + img_tok // 2)
    half_chunks = chunks // 2

    me_s = lax.axis_index("seq")
    me_h = lax.axis_index("head")
    y, core = me_h // 2, me_h % 2
    me_z, me_x = me_s // nx, me_s % nx

    def wrap_y(v):
        return lax.rem(v + 2 * ny, ny)

    def on_ring(v):
        return (me_s, wrap_y(v) * 2 + core)

    sibling = (me_s, y * 2 + 1 - core)

    def remote(src, dst, ssem, rsem, to):
        return pltpu.make_async_remote_copy(
            src_ref=src, dst_ref=dst, send_sem=ssem, recv_sem=rsem, device_id=to, device_id_type=MESH
        )

    loads = [(q_hbm, q_v), (k_hbm, k_v), (v_hbm, v_v), (text_hbm, text_v), (kvw_hbm, kvw_v), (w_hbm, w_v)]
    copies = [pltpu.make_async_copy(a, b, load_sem.at[i]) for i, (a, b) in enumerate(loads)]
    for c in copies:
        c.start()

    barrier = pltpu.get_barrier_semaphore()

    @pl.loop(1, n_seq)
    def _(i):
        pl.semaphore_signal(
            barrier, inc=1, device_id=(lax.rem(me_s + i, n_seq), me_h), device_id_type=MESH
        )

    for d in range(1, ny):
        pl.semaphore_signal(barrier, inc=1, device_id=on_ring(y + d), device_id_type=MESH)
    pl.semaphore_signal(barrier, inc=1, device_id=sibling, device_id_type=MESH)

    def peer_of(n, sign):
        j = n >> log2(KEEP)
        m = j >> log2(nx)
        mag = (nz - m) >> 1
        dz = jnp.where((m & 1) == 0, mag, -mag)
        dx = (nx - 1) - (j & (nx - 1))
        return (((me_z + sign * dz) & (nz - 1)) << log2(nx)) + ((me_x + sign * dx) & (nx - 1))

    def first_position(start):
        return start + ((me_s - start) & (n_seq - 1))

    my_start = slot_s[me_s] * example_len + offset_s[me_s]
    n_q = lax.broadcasted_iota(jnp.int32, (img_tok, img_tok), 0)
    col_q = lax.broadcasted_iota(jnp.int32, (img_tok, img_tok), 1)
    token = ((peer_of(n_q, 1) - my_start) & (n_seq - 1)) + n_seq * (n_q & (KEEP - 1))
    order = one_hot(col_q == token)
    side = PACK * nj
    row_p = lax.broadcasted_iota(jnp.int32, (side, side), 0)
    col_p = lax.broadcasted_iota(jnp.int32, (side, side), 1)

    def packed_from(q):
        return ((q >> log2(KEEP)) & (FEAT // 128 - 1)) * rc + (q >> log2(PACK)) * KEEP + (q & (KEEP - 1))

    pack_m[...] = one_hot(col_p == packed_from(row_p))
    unpack_m[...] = one_hot(row_p == packed_from(col_p))

    copies[0].wait()
    qp[...] = dot(order, q_v[...]).astype(BF16)
    copies[1].wait()
    copies[2].wait()

    def attend(r):
        rows = pl.ds(pl.multiple_of(r * rc, rc), rc)
        for h in range(HEADS):
            cols = slice(h * VIT_HD, (h + 1) * VIT_HD)
            scores = lax.dot_general(
                qp[rows, cols], k_v[:, cols], (((1,), (1,)), ((), ())), preferred_element_type=F32
            ) / math.sqrt(VIT_HD)
            weights = jnp.exp(scores)
            attention = (weights / jnp.sum(weights, axis=-1, keepdims=True)).astype(BF16)
            att[r, y, core * HEADS + h] = dot(attention, v_v[:, cols]).astype(BF16)

    mine = pl.ds(core * HEADS, HEADS)

    def ring_copy(r, way, hop):
        origin = wrap_y(y - (hop - 1)) if way == 0 else wrap_y(y + (hop - 1))
        block = att.at[r, origin, mine]
        to = on_ring(y + 1) if way == 0 else on_ring(y - 1)
        return remote(block, block, ring_send.at[r, way, hop - 1], ring_recv.at[r, way, hop - 1], to)

    def ring_arrival(r, way, hop):
        origin = wrap_y(y - hop) if way == 0 else wrap_y(y + hop)
        block = att.at[r, origin, mine]
        return remote(block, block, ring_send.at[r, way, hop - 1], ring_recv.at[r, way, hop - 1], sibling)

    def origin_of(slot):
        return wrap_y(y - slot) if slot <= hops else wrap_y(y + (slot - hops))

    def sib_copy(r, slot):
        block = att.at[r, origin_of(slot), mine]
        return remote(block, block, sib_send.at[r, slot], sib_recv.at[r, slot], sibling)

    def sib_arrival(r, slot):
        block = att.at[r, origin_of(slot), pl.ds((1 - core) * HEADS, HEADS)]
        return remote(block, block, sib_send.at[r, slot], sib_recv.at[r, slot], sibling)

    width = 2 * HEADS * VIT_HD

    def accumulate(r, slot):
        sib_arrival(r, slot).wait_recv()
        o = origin_of(slot)
        lhs = jnp.concatenate([att[r, o, i] for i in range(2 * HEADS)], axis=1)
        acc[r] += dot(lhs, w_v[pl.ds(pl.multiple_of(o * width, width), width), :])

    def farthest_way(r):
        return r % 2

    def far_slot_ops(r, op):
        for way in (0, 1):
            @pl.when(farthest_way(r) == way)
            def _():
                op(way)

    def peer_scalar(j):
        m = j // nx
        mag = (nz - m) // 2
        dz = jnp.where(m % 2 == 0, mag, -mag)
        dx = (nx - 1) - j % nx
        return lax.rem(me_z + dz + nz, nz) * nx + lax.rem(me_x + dx, nx)

    def send_chunk(r):
        stacked = jnp.concatenate(
            [acc[r, :, f * 128:(f + 1) * 128].astype(BF16) for f in range(FEAT // 128)], axis=0
        )
        packed = dot(pack_m[...], stacked).astype(BF16)
        send_b[r] = packed.reshape(nj, PACK, 128)

        @pl.when(r == chunks - 1)
        def _():
            recv_b[chunks - 1, nj - 1] = send_b[chunks - 1, nj - 1]

        @pl.loop(0, nj - jnp.where(r == chunks - 1, 1, 0))
        def _(jj):
            remote(
                send_b.at[r, jj], recv_b.at[r, jj], a2a_send.at[r], a2a_recv.at[r],
                (peer_scalar(r * nj + jj), me_h),
            ).start()

    def a2a_all(r):
        n = nj - 1 if r == chunks - 1 else nj
        return remote(
            send_b.at[r, pl.ds(0, n)], recv_b.at[r, pl.ds(0, n)], a2a_send.at[r], a2a_recv.at[r], sibling
        )

    def take_chunk(r):
        a2a_all(r).wait_recv()
        stacked = dot(unpack_m[...], recv_b[r].reshape(nj * PACK, 128)).astype(BF16)
        tok[r * rc:(r + 1) * rc, :] = jnp.concatenate(
            [stacked[f * rc:(f + 1) * rc] for f in range(FEAT // 128)], axis=1
        )

    def kv_partial(g, rows_in):
        n = group_rows[g]
        widened = rows_in.astype(F32)
        squares = jnp.sum(widened * widened, axis=1, keepdims=True)
        scaled = (widened * gain[...]).astype(BF16)
        sums = dot(scaled, kvw_v[...])
        base = slice(group_base[g], group_base[g] + n)
        for half in (0, 1):
            halves[half, base, :KV_HD] = sums[:, half * KV_HD:(half + 1) * KV_HD]
            halves[half, base, KV_HD:] = jnp.broadcast_to(squares, (n, 128))
        half_copy(g).start()

    def half_copy(g):
        base = pl.ds(group_base[g], group_rows[g])
        return remote(
            halves.at[1 - core, base], sib_b.at[base], half_send.at[g], half_recv.at[g], sibling
        )

    def rs_copy(g, d):
        rr = group_rows[g] // ny
        at = pl.multiple_of(group_base[g] + wrap_y(y + d) * rr, rr)
        at_recv = (group_base[g] // ny) * (ny - 1) + (d - 1) * rr
        return remote(
            rs_send.at[pl.ds(at, rr)], rs_recv.at[pl.ds(at_recv, rr)], rs_ssem.at[g, d - 1], rs_rsem.at[g, d - 1],
            on_ring(y + d),
        )

    def kv_scatter(g):
        half_copy(g).wait_recv()
        n = group_rows[g]
        base = slice(group_base[g], group_base[g] + n)
        chip = halves[core, base, :] + sib_b[base, :]
        squares = chip[:, KV_HD:]
        high = squares.astype(BF16)
        low = (squares - high.astype(F32)).astype(BF16)
        lane = lax.broadcasted_iota(jnp.int32, (n, 128), 1)
        rs_send[base, :KV_HD] = chip[:, :KV_HD].astype(BF16)
        rs_send[base, KV_HD:] = jnp.where(lane < 64, high.astype(F32), low.astype(F32)).astype(BF16)
        for d in range(1, ny):
            rs_copy(g, d).start()

    def own_rows(g):
        rr = group_rows[g] // ny
        return pl.ds(pl.multiple_of(group_base[g] + y * rr, rr), rr)

    def ag_copy(g, d):
        block = kvfin.at[core, own_rows(g)]
        return remote(block, block, ag_ssem.at[g, d - 1], ag_rsem.at[g, d - 1], on_ring(y + d))

    def ag_arrival(g, d):
        rr = group_rows[g] // ny
        at = pl.multiple_of(group_base[g] + wrap_y(y - d) * rr, rr)
        block = kvfin.at[core, pl.ds(at, rr)]
        return remote(block, block, ag_ssem.at[g, d - 1], ag_rsem.at[g, d - 1], sibling)

    def fwd_copy(g):
        block = kvfin.at[core, pl.ds(group_base[g], group_rows[g])]
        return remote(block, block, fwd_send.at[g], fwd_recv.at[g], sibling)

    def fwd_arrival(g):
        block = kvfin.at[1 - core, pl.ds(group_base[g], group_rows[g])]
        return remote(block, block, fwd_send.at[g], fwd_recv.at[g], sibling)

    def kv_finish(g):
        rr = group_rows[g] // ny
        total = rs_send[own_rows(g), :].astype(F32)
        for d in range(1, ny):
            rs_copy(g, d).wait_recv()
            at = (group_base[g] // ny) * (ny - 1) + (d - 1) * rr
            total += rs_recv[at:at + rr, :].astype(F32)
        squares = total[:, KV_HD:KV_HD + 1] + total[:, KV_HD + 64:KV_HD + 65]
        projected = total[:, :KV_HD] * (1.0 / jnp.sqrt(squares / d_model + 1e-06))
        first, second = projected[:, :128], projected[:, 128:]
        tb = group_base[g] // ny
        cosine, sine = trig[0, tb:tb + rr, :], trig[1, tb:tb + rr, :]
        kvfin[core, own_rows(g), :128] = (first * cosine - second * sine).astype(BF16)
        kvfin[core, own_rows(g), 128:] = (second * cosine + first * sine).astype(BF16)
        for d in range(1, ny):
            ag_copy(g, d).start()

    def kv_forward(g):
        for d in range(1, ny):
            ag_arrival(g, d).wait_recv()
        fwd_copy(g).start()

    def kv_place(g):
        fwd_arrival(g).wait_recv()
        n = group_rows[g]
        base = slice(group_base[g], group_base[g] + n)
        hot = one_hot(lax.broadcasted_iota(jnp.int32, (local_rows, n), 0) == place[:, base])
        return dot(hot, jnp.concatenate([kvfin[0, base, :], kvfin[1, base, :]], axis=1))

    def prepare():
        n_lane = lax.broadcasted_iota(jnp.int32, (n_seq, img_tok), 1)
        i_sub = lax.broadcasted_iota(jnp.int32, (n_seq, img_tok), 0)
        start_c = slot_col[...] * example_len + offset_col[...]
        first_c = (first_position(start_c) >> log2(n_seq)).astype(F32)
        keep_l = lax.broadcasted_iota(jnp.int32, (1, img_tok), 1)
        row_i = jnp.sum(jnp.where(i_sub == peer_of(n_lane, -1), first_c, 0.0), axis=0, keepdims=True)
        place[:, img_tok:] = row_i.astype(jnp.int32) + (keep_l & (KEEP - 1))
        row_t = jnp.sum(jnp.where(slot_col[...] == (n_lane >> log2(KEEP)), first_c, 0.0), axis=0, keepdims=True)
        place[:, :img_tok] = text_row(row_t.astype(jnp.int32), keep_l)
        n_sub = lax.broadcasted_iota(jnp.int32, (img_tok, n_seq), 0)
        i_lane = lax.broadcasted_iota(jnp.int32, (img_tok, n_seq), 1)
        start_r = slot_row[...] * example_len + offset_row[...]
        first_r = (first_position(start_r) >> log2(n_seq)).astype(F32)
        keep_s = lax.broadcasted_iota(jnp.int32, (img_tok, 1), 0)
        row_i = jnp.sum(jnp.where(i_lane == peer_of(n_sub, -1), first_r, 0.0), axis=1, keepdims=True)
        row_i = row_i.astype(jnp.int32) + (keep_s & (KEEP - 1))
        row_t = jnp.sum(jnp.where(slot_row[...] == (n_sub >> log2(KEEP)), first_r, 0.0), axis=1, keepdims=True)
        row_t = text_row(row_t.astype(jnp.int32), keep_s)
        pos[:img_tok, :] = row_t
        pos[img_tok:, :] = row_i
        hot = one_hot(lax.broadcasted_iota(jnp.int32, (img_tok, local_rows), 1) == row_t)
        copies[3].wait()
        copies[4].wait()
        kv_partial(0, dot(hot, text_v[...]))
        for g in range(3):
            rr = group_rows[g] // ny
            tb = group_base[g] // ny
            angles = (pos[own_rows(g), :] * n_seq + me_s).astype(F32) * freq[...]
            keys = core == 0
            trig[0, tb:tb + rr, :] = jnp.where(keys, jnp.cos(angles), 1.0)
            trig[1, tb:tb + rr, :] = jnp.where(keys, jnp.sin(angles), 0.0)

    def text_row(first, n):
        e, m = n >> log2(KEEP), n & (KEEP - 1)
        row = e * per_example + m
        return jnp.where(row >= first, row + KEEP, row)

    acc[...] = jnp.zeros_like(acc)
    pl.semaphore_wait(barrier, n_seq - 1 + ny)

    def step(r, s):
        if s == 0:
            attend(r)
            for way in (0, 1):
                if hops > 1:
                    ring_copy(r, way, 1).start()
            if hops == 1:
                far_slot_ops(r, lambda way: ring_copy(r, way, 1).start())
            sib_copy(r, 0).start()
        if 1 <= s < hops:
            for way in (0, 1):
                ring_arrival(r, way, s).wait_recv()
                if s + 1 < hops:
                    ring_copy(r, way, s + 1).start()
                else:
                    @pl.when(farthest_way(r) == way)
                    def _():
                        ring_copy(r, way, s + 1).start()
                sib_copy(r, s if way == 0 else hops + s).start()
        if s == hops:
            far_slot_ops(r, lambda way: ring_arrival(r, way, s).wait_recv())
            sib_copy(r, hops).start()
        if s == 1:
            accumulate(r, 0)
        if 2 <= s <= hops:
            accumulate(r, s - 1)
            accumulate(r, hops + s - 1)
        if s == hops + 1:
            accumulate(r, hops)
            send_chunk(r)

    depth = (hops + 3) // 2
    ticks = chunks + depth - 1

    @pl.loop(0, ticks)
    def _(tt):
        for par in (0, 1):
            for back in reversed(range(depth)):
                s = 2 * back + par
                if s > hops + 1:
                    continue
                r = tt - back

                @pl.when((r >= 0) & (r < chunks))
                def _():
                    step(r, s)

            if par == 0:
                @pl.when(tt == 0)
                def _():
                    prepare()
                    copies[5].wait()

                @pl.when(tt == 1)
                def _():
                    kv_scatter(0)

                @pl.when(tt == 2)
                def _():
                    kv_finish(0)

                @pl.when(tt == ticks - 2)
                def _():
                    kv_forward(0)

    for r in range(half_chunks):
        take_chunk(r)
    kv_partial(1, tok[:img_tok // 2, :])
    kv_acc[...] = kv_place(0)
    kv_scatter(1)
    for r in range(half_chunks, chunks):
        take_chunk(r)
    kv_partial(2, tok[img_tok // 2:, :])
    kv_finish(1)
    hot = one_hot(lax.broadcasted_iota(jnp.int32, (local_rows, img_tok), 0) == place[:, img_tok:])
    kv_scatter(2)
    is_image = jnp.sum(hot.astype(F32), axis=1, keepdims=True)
    merged_v[...] = jnp.where(is_image > 0.5, dot(hot, tok[...]), text_v[...].astype(F32)).astype(BF16)
    merged_out = pltpu.make_async_copy(merged_v, merged_hbm, out_sem.at[0])
    merged_out.start()
    kv_forward(1)
    kv_finish(2)
    kv_acc[...] += kv_place(1)
    kv_forward(2)
    kv_v[...] = (kv_acc[...] + kv_place(2)).astype(BF16)
    kv_out = pltpu.make_async_copy(kv_v, kv_hbm, out_sem.at[1])
    kv_out.start()

    @pl.loop(0, chunks)
    def _(r):
        for way in (0, 1):
            for hop in range(1, hops):
                ring_copy(r, way, hop).wait_send()
        far_slot_ops(r, lambda way: ring_copy(r, way, hops).wait_send())
        for slot in range(2 * hops):
            sib_copy(r, slot).wait_send()

    for r in range(chunks):
        a2a_all(r).wait_send()
    for g in range(3):
        half_copy(g).wait_send()
        for d in range(1, ny):
            rs_copy(g, d).wait_send()
            ag_copy(g, d).wait_send()
        fwd_copy(g).wait_send()
    merged_out.wait()
    kv_out.wait()


def on_device(
    nx,
    vit_query,
    vit_key,
    vit_value,
    image_proj,
    image_slot,
    image_offset,
    text_embed,
    norm_gain,
    kv_weight,
):
    n_seq, n_head = lax.axis_size("seq"), lax.axis_size("head")
    nz, ny = n_seq // nx, n_head // 2
    img_tok, local_rows = vit_query.shape[0], text_embed.shape[0]
    chunks = min(4, nz)
    hops = ny // 2
    d_model = n_head * FEAT
    rows = 2 * img_tok
    nj = img_tok // chunks // KEEP
    exponent = np.arange(KV_HD // 2, dtype=np.float32) * np.float32(2.0 / KV_HD)
    freq = jnp.power(jnp.float32(10000.0), -jnp.asarray(exponent))[None, :]
    sizes = (n_seq, nz, nx, ny, chunks, img_tok, local_rows, d_model)
    hbm = pl.BlockSpec(memory_space=pltpu.HBM)
    vmem = pl.BlockSpec(memory_space=pltpu.VMEM)
    smem = pl.BlockSpec(memory_space=pltpu.SMEM)
    dma = pltpu.SemaphoreType.DMA
    merged, keys_values = pl.pallas_call(
        functools.partial(kernel, sizes),
        out_shape=(
            jax.ShapeDtypeStruct((local_rows, FEAT), BF16),
            jax.ShapeDtypeStruct((local_rows, KV), BF16),
        ),
        in_specs=[hbm] * 6 + [vmem, smem, smem] + [vmem] * 5,
        out_specs=(hbm, hbm),
        scratch_shapes=[
            pltpu.VMEM(vit_query.shape, BF16),
            pltpu.VMEM(vit_query.shape, BF16),
            pltpu.VMEM(vit_query.shape, BF16),
            pltpu.VMEM(image_proj.shape, BF16),
            pltpu.VMEM((local_rows, FEAT), BF16),
            pltpu.VMEM(kv_weight.shape, BF16),
            pltpu.VMEM(vit_query.shape, BF16),
            pltpu.VMEM((chunks, ny, 2 * HEADS, img_tok // chunks, VIT_HD), BF16),
            pltpu.VMEM((chunks, img_tok // chunks, FEAT), F32),
            pltpu.VMEM((PACK * nj, PACK * nj), BF16),
            pltpu.VMEM((PACK * nj, PACK * nj), BF16),
            pltpu.VMEM((chunks, nj, PACK, 128), BF16),
            pltpu.VMEM((chunks, nj, PACK, 128), BF16),
            pltpu.VMEM((img_tok, FEAT), BF16),
            pltpu.VMEM((1, rows), jnp.int32),
            pltpu.VMEM((rows, 1), jnp.int32),
            pltpu.VMEM((2, rows // ny, 128), F32),
            pltpu.VMEM((2, rows, SIDE), F32),
            pltpu.VMEM((rows, SIDE), F32),
            pltpu.VMEM((rows, SIDE), BF16),
            pltpu.VMEM((rows // ny * (ny - 1), SIDE), BF16),
            pltpu.VMEM((2, rows, KV_HD), BF16),
            pltpu.VMEM((local_rows, FEAT), BF16),
            pltpu.VMEM((local_rows, KV), BF16),
            pltpu.VMEM((local_rows, KV), F32),
            dma((6,)),
            dma((2,)),
            dma((chunks, 2, hops)),
            dma((chunks, 2, hops)),
            dma((chunks, 2 * hops)),
            dma((chunks, 2 * hops)),
            dma((chunks,)),
            dma((chunks,)),
            dma((3,)),
            dma((3,)),
            dma((3, ny - 1)),
            dma((3, ny - 1)),
            dma((3, ny - 1)),
            dma((3, ny - 1)),
            dma((3,)),
            dma((3,)),
        ],
        compiler_params=pltpu.CompilerParams(
            collective_id=0, has_side_effects=True, vmem_limit_bytes=48 * 1024 * 1024
        ),
        cost_estimate=pl.CostEstimate(flops=2 * 10**9, bytes_accessed=10**7, transcendentals=200000),
    )(
        vit_query,
        vit_key,
        vit_value,
        image_proj,
        text_embed.reshape(local_rows, FEAT),
        kv_weight,
        norm_gain[None, :],
        image_slot,
        image_offset,
        image_slot[None, :],
        image_offset[None, :],
        image_slot[:, None],
        image_offset[:, None],
        freq,
    )
    return merged[:, None, :], keys_values[:, None, :]


def solution(mesh):
    placed = (
        P("seq", "head"),
        P("seq", "head"),
        P("seq", "head"),
        P(None, "head"),
        P(),
        P(),
        P(None, "seq", "head"),
        P("head"),
        P("head", None),
    )
    return jax.shard_map(
        functools.partial(on_device, 4 if mesh.shape["seq"] % 16 == 0 else 2),
        mesh=mesh,
        in_specs=placed,
        out_specs=(P(None, "seq", "head"), P(None, "seq", None)),
        check_vma=False,
    )
```

```python
import functools
import math

import jax
import jax.numpy as jnp
import numpy as np
from jax import lax
from jax.experimental import pallas as pl
from jax.experimental.pallas import tpu as pltpu
from jax.sharding import PartitionSpec as P

KV_HD = 256
VIT_HD = 128
HEADS = 3
FEAT = 512
KV = 512
KEEP = 4
PACK = FEAT // 128 * KEEP
SIDE = KV_HD + 128
MESH = pl.DeviceIdType.MESH
F32 = jnp.float32
BF16 = jnp.bfloat16


def log2(n):
    return n.bit_length() - 1


def dot(a, b):
    return jnp.dot(a, b, preferred_element_type=F32)


def one_hot(hits):
    return jnp.where(hits, 1.0, 0.0).astype(BF16)


def kernel(
    sizes,
    q_hbm, k_hbm, v_hbm, w_hbm, text_hbm, kvw_hbm, gain_hbm, slot_hbm, offset_hbm, freq_hbm,
    merged_hbm, kv_hbm,
    q_v, k_v, v_v, w_v, text_v, kvw_v, gain, slot_row, offset_row, freq, qp, att, acc, pack_m, unpack_m,
    send_b, recv_b, src_tok, tok, place, pos, trig, turn, halves, sib_b, rs_send, rs_recv, kvfin,
    img_half, img_sib, img_rs, img_rr, kvs, kvr, kv_img, merged_v, kv_v, kv_acc,
    load_sem, out_sem, ring_send, ring_recv, sib_send, sib_recv, far_recv, a2a_send, a2a_recv,
    half_send, half_recv, rs_ssem, rs_rsem, ag_ssem, ag_rsem, fwd_send, fwd_recv, kva_send, kva_recv,
):
    n_seq, nz, nx, ny, chunks, img_tok, example_len, d_model = sizes
    hops = ny // 2
    rc = img_tok // chunks
    nj = rc // KEEP
    local_rows = example_len
    per_example = example_len // n_seq
    text_rr = img_tok // ny
    half_rows = 2 * rc // 2
    mine_rows = half_rows // ny

    me_s = lax.axis_index("seq")
    me_h = lax.axis_index("head")
    y, core = me_h // 2, me_h % 2
    me_z, me_x = me_s // nx, me_s % nx

    def wrap_y(v):
        return lax.rem(v + 2 * ny, ny)

    def on_ring(v):
        return (me_s, wrap_y(v) * 2 + core)

    sibling = (me_s, y * 2 + 1 - core)

    def remote(src, dst, ssem, rsem, to):
        return pltpu.make_async_remote_copy(
            src_ref=src, dst_ref=dst, send_sem=ssem, recv_sem=rsem, device_id=to, device_id_type=MESH
        )

    loads = [
        (slot_hbm, slot_row), (offset_hbm, offset_row), (q_hbm, q_v), (k_hbm, k_v), (v_hbm, v_v),
        (gain_hbm, gain), (freq_hbm, freq), (text_hbm, text_v), (kvw_hbm, kvw_v), (w_hbm, w_v),
    ]
    copies = [pltpu.make_async_copy(a, b, load_sem.at[i]) for i, (a, b) in enumerate(loads)]
    for c in copies:
        c.start()

    barrier = pltpu.get_barrier_semaphore()

    @pl.loop(1, n_seq)
    def _(i):
        pl.semaphore_signal(
            barrier, inc=1, device_id=(lax.rem(me_s + i, n_seq), me_h), device_id_type=MESH
        )

    for d in range(1, ny):
        pl.semaphore_signal(barrier, inc=1, device_id=on_ring(y + d), device_id_type=MESH)
    pl.semaphore_signal(barrier, inc=1, device_id=sibling, device_id_type=MESH)

    def peer_of(n, sign):
        j = n >> log2(KEEP)
        m = j >> log2(nx)
        mag = (nz - m) >> 1
        dz = jnp.where((m & 1) == 0, mag, -mag)
        dx = (nx - 1) - (j & (nx - 1))
        return (((me_z + sign * dz) & (nz - 1)) << log2(nx)) + ((me_x + sign * dx) & (nx - 1))

    def first_position(start):
        return start + ((me_s - start) & (n_seq - 1))

    copies[0].wait()
    copies[1].wait()
    start_r = (slot_row[...] * example_len + offset_row[...]).astype(F32)
    lanes = lax.broadcasted_iota(jnp.int32, (1, n_seq), 1)
    my_start = jnp.sum(jnp.where(lanes == me_s, start_r, 0.0), axis=1, keepdims=True).astype(jnp.int32)
    n_q = lax.broadcasted_iota(jnp.int32, (img_tok, img_tok), 0)
    col_q = lax.broadcasted_iota(jnp.int32, (img_tok, img_tok), 1)

    def token_of(n):
        return ((peer_of(n, 1) - my_start) & (n_seq - 1)) + n_seq * (n & (KEEP - 1))

    order = one_hot(col_q == token_of(n_q))
    side = PACK * nj
    row_p = lax.broadcasted_iota(jnp.int32, (side, side), 0)
    col_p = lax.broadcasted_iota(jnp.int32, (side, side), 1)

    def packed_from(q):
        return ((q >> log2(KEEP)) & (FEAT // 128 - 1)) * rc + (q >> log2(PACK)) * KEEP + (q & (KEEP - 1))

    pack_m[...] = one_hot(col_p == packed_from(row_p))
    unpack_m[...] = one_hot(row_p == packed_from(col_p))

    copies[2].wait()
    qp[...] = dot(order, q_v[...]).astype(BF16)
    copies[3].wait()
    copies[4].wait()

    def attend(r):
        rows = pl.ds(pl.multiple_of(r * rc, rc), rc)
        for h in range(HEADS):
            cols = slice(h * VIT_HD, (h + 1) * VIT_HD)
            scores = lax.dot_general(
                qp[rows, cols], k_v[:, cols], (((1,), (1,)), ((), ())), preferred_element_type=F32
            ) / math.sqrt(VIT_HD)
            weights = jnp.exp(scores)
            attention = (weights / jnp.sum(weights, axis=-1, keepdims=True)).astype(BF16)
            att[y, core * HEADS + h, rows, :] = dot(attention, v_v[:, cols]).astype(BF16)

    def block_of(r, origin, side_core):
        rows = pl.ds(pl.multiple_of(r * rc, rc), rc)
        return att.at[origin, pl.ds(side_core * HEADS, HEADS), rows]

    def ring_copy(r, way, hop):
        origin = wrap_y(y - (hop - 1)) if way == 0 else wrap_y(y + (hop - 1))
        block = block_of(r, origin, core)
        to = on_ring(y + 1) if way == 0 else on_ring(y - 1)
        return remote(block, block, ring_send.at[way, hop - 1], ring_recv.at[r, way, hop - 1], to)

    def ring_arrival(r, way, hop):
        origin = wrap_y(y - hop) if way == 0 else wrap_y(y + hop)
        block = block_of(r, origin, core)
        return remote(block, block, ring_send.at[way, hop - 1], ring_recv.at[r, way, hop - 1], sibling)

    def origin_of(slot):
        return wrap_y(y - slot) if slot <= hops else wrap_y(y + (slot - hops))

    def sib_recv_sem(r, slot):
        return far_recv.at[r] if slot == hops else sib_recv.at[slot]

    def sib_copy(r, slot):
        block = block_of(r, origin_of(slot), core)
        return remote(block, block, sib_send.at[slot], sib_recv_sem(r, slot), sibling)

    def sib_arrival(r, slot):
        block = block_of(r, origin_of(slot), 1 - core)
        return remote(block, block, sib_send.at[slot], sib_recv_sem(r, slot), sibling)

    def sib_all(slot, side_core):
        block = att.at[origin_of(slot), pl.ds(side_core * HEADS, HEADS)]
        return remote(block, block, sib_send.at[slot], sib_recv.at[slot], sibling)

    width = 2 * HEADS * VIT_HD

    def weights_of(o):
        return w_v[pl.ds(pl.multiple_of(o * width, width), width), :]

    def accumulate(slot, first=False):
        sib_all(slot, 1 - core).wait_recv()
        o = origin_of(slot)
        lhs = jnp.concatenate([att[o, i] for i in range(2 * HEADS)], axis=1)
        product = dot(lhs, weights_of(o))
        if first:
            acc[...] = product
        else:
            acc[...] += product

    def farthest_way(r):
        return r % 2

    def far_slot_ops(r, op):
        for way in (0, 1):
            @pl.when(farthest_way(r) == way)
            def _():
                op(way)

    def peer_scalar(j):
        m = j // nx
        mag = (nz - m) // 2
        dz = jnp.where(m % 2 == 0, mag, -mag)
        dx = (nx - 1) - j % nx
        return lax.rem(me_z + dz + nz, nz) * nx + lax.rem(me_x + dx, nx)

    def send_chunk(r):
        sib_arrival(r, hops).wait_recv()
        o = origin_of(hops)
        rows = pl.ds(pl.multiple_of(r * rc, rc), rc)
        lhs = jnp.concatenate([att[o, i, rows, :] for i in range(2 * HEADS)], axis=1)
        total = (acc[rows, :] + dot(lhs, weights_of(o))).astype(BF16)
        src_tok[rows, :] = total
        stacked = jnp.concatenate(
            [total[:, f * 128:(f + 1) * 128] for f in range(FEAT // 128)], axis=0
        )
        packed = dot(pack_m[...], stacked).astype(BF16)
        send_b[r] = packed.reshape(nj, PACK, 128)

        @pl.when(r == chunks - 1)
        def _():
            recv_b[chunks - 1, nj - 1] = send_b[chunks - 1, nj - 1]

        @pl.loop(0, nj - jnp.where(r == chunks - 1, 1, 0))
        def _(jj):
            remote(
                send_b.at[r, jj], recv_b.at[r, jj], a2a_send.at[r], a2a_recv.at[r],
                (peer_scalar(r * nj + jj), me_h),
            ).start()

    def a2a_all(r):
        n = nj - 1 if r == chunks - 1 else nj
        return remote(
            send_b.at[r, pl.ds(0, n)], recv_b.at[r, pl.ds(0, n)], a2a_send.at[r], a2a_recv.at[r], sibling
        )

    def unpack(blocks):
        stacked = dot(unpack_m[...], blocks).astype(BF16)
        return jnp.concatenate([stacked[f * rc:(f + 1) * rc] for f in range(FEAT // 128)], axis=1)

    def take_chunk(r):
        a2a_all(r).wait_recv()
        tok[r * rc:(r + 1) * rc, :] = unpack(recv_b[r].reshape(nj * PACK, 128))

    def kv_sums(rows_in):
        widened = rows_in.astype(F32)
        squares = jnp.sum(widened * widened, axis=1, keepdims=True)
        return dot((widened * gain[...]).astype(BF16), kvw_v[...]), squares

    def two_parts(squares):
        high = squares.astype(BF16).astype(F32)
        return high, squares - high

    def inverse(squares):
        return 1.0 / jnp.sqrt(squares / d_model + 1e-06)

    def half_copy():
        return remote(halves.at[1 - core], sib_b, half_send.at[0], half_recv.at[0], sibling)

    def text_partial(rows_in):
        sums, squares = kv_sums(rows_in)
        for half in (0, 1):
            halves[half, :, :KV_HD] = sums[:, half * KV_HD:(half + 1) * KV_HD]
            halves[half, :, KV_HD:] = jnp.broadcast_to(squares, (img_tok, 128))
        half_copy().start()

    def text_rs(d):
        at = pl.multiple_of(wrap_y(y + d) * text_rr, text_rr)
        return remote(
            rs_send.at[pl.ds(at, text_rr)], rs_recv.at[pl.ds((d - 1) * text_rr, text_rr)],
            rs_ssem.at[0], rs_rsem.at[0], on_ring(y + d),
        )

    def text_rs_all():
        everything = rs_recv.at[pl.ds(0, (ny - 1) * text_rr)]
        return remote(everything, everything, rs_ssem.at[0], rs_rsem.at[0], sibling)

    def text_scatter():
        half_copy().wait_recv()
        chip = halves[core] + sib_b[...]
        high, low = two_parts(chip[:, KV_HD:])
        lane = lax.broadcasted_iota(jnp.int32, (img_tok, 128), 1)
        rs_send[:, :KV_HD] = chip[:, :KV_HD].astype(BF16)
        rs_send[:, KV_HD:] = jnp.where(lane < 64, high, low).astype(BF16)
        for d in range(1, ny):
            text_rs(d).start()

    def text_rows_of(o):
        return pl.ds(pl.multiple_of(o * text_rr, text_rr), text_rr)

    def text_ag(d):
        block = kvfin.at[core, text_rows_of(y)]
        return remote(block, block, ag_ssem.at[0], ag_rsem.at[0, d - 1], on_ring(y + d))

    def text_ag_arrival(d):
        block = kvfin.at[core, text_rows_of(wrap_y(y - d))]
        return remote(block, block, ag_ssem.at[0], ag_rsem.at[0, d - 1], sibling)

    def text_ag_all():
        block = kvfin.at[core, pl.ds(0, (ny - 1) * text_rr)]
        return remote(block, block, ag_ssem.at[0], ag_rsem.at[0, 0], sibling)

    def text_fwd(side_core):
        block = kvfin.at[side_core]
        return remote(block, block, fwd_send.at[0], fwd_recv.at[0], sibling)

    def text_finish():
        text_rs_all().wait_recv()
        total = rs_send[text_rows_of(y), :].astype(F32)
        for d in range(1, ny):
            total += rs_recv[(d - 1) * text_rr:d * text_rr, :].astype(F32)
        squares = total[:, KV_HD:KV_HD + 1] + total[:, KV_HD + 64:KV_HD + 65]
        projected = total[:, :KV_HD] * inverse(squares)
        first, second = projected[:, :128], projected[:, 128:]
        kvfin[core, text_rows_of(y), :128] = (first * trig[0] - second * trig[1]).astype(BF16)
        kvfin[core, text_rows_of(y), 128:] = (second * trig[0] + first * trig[1]).astype(BF16)
        for d in range(1, ny):
            text_ag(d).start()

    def text_forward():
        for d in range(1, ny):
            text_ag_arrival(d).wait_recv()
        text_fwd(core).start()

    def img_half_copy(g):
        return remote(img_half.at[g, 1 - core], img_sib.at[g], half_send.at[1 + g], half_recv.at[1 + g], sibling)

    def img_partial(g):
        sums, squares = kv_sums(src_tok[pl.ds(pl.multiple_of(g * 2 * rc, 2 * rc), 2 * rc), :])
        for half in (0, 1):
            rows = slice(half * half_rows, (half + 1) * half_rows)
            img_half[g, half, :, :KV] = sums[rows]
            img_half[g, half, :, KV:] = jnp.broadcast_to(squares[rows], (half_rows, 128))
        img_half_copy(g).start()

    def img_scatter(g):
        img_half_copy(g).wait_recv()
        chip = img_half[g, core] + img_sib[g]
        sums = chip[:, :KV].reshape(ny, mine_rows, KV)
        high, low = two_parts(chip[:, KV:].reshape(ny, mine_rows, 128))
        img_rs[g, :, :, :KV_HD] = jnp.concatenate([sums[:, :, :KV_HD], sums[:, :, KV_HD:]], axis=1).astype(BF16)
        img_rs[g, :, :, KV_HD:] = jnp.concatenate([high, low], axis=1).astype(BF16)
        for d in range(1, ny):
            remote(
                img_rs.at[g, wrap_y(y + d)], img_rr.at[g, d - 1], rs_ssem.at[1 + g], rs_rsem.at[1 + g],
                on_ring(y + d),
            ).start()

    def img_rs_all(g):
        return remote(img_rr.at[g], img_rr.at[g], rs_ssem.at[1 + g], rs_rsem.at[1 + g], sibling)

    def img_finish(g):
        img_rs_all(g).wait_recv()
        total = img_rs[g, y].astype(F32)
        for d in range(ny - 1):
            total += img_rr[g, d].astype(F32)
        m = mine_rows
        scale = inverse(total[:m, KV_HD:KV_HD + 1] + total[m:, KV_HD:KV_HD + 1])
        keys, values = total[:m, :KV_HD] * scale, total[m:, :KV_HD] * scale
        first, second = keys[:, :128], keys[:, 128:]
        cosine, sine = turn[g, 0], turn[g, 1]
        parts = (
            first * cosine - second * sine, second * cosine + first * sine, values[:, :128], values[:, 128:],
        )
        swapped = [pltpu.roll(part, KEEP, axis=0) for part in parts]
        lower = lax.broadcasted_iota(jnp.int32, (m, 128), 0) < KEEP
        kvs[g, 0] = jnp.concatenate(
            [jnp.where(lower, parts[0], swapped[1]), jnp.where(lower, parts[2], swapped[3])], axis=0
        ).astype(BF16)
        kvs[g, 1] = jnp.concatenate(
            [jnp.where(lower, swapped[0], parts[1]), jnp.where(lower, swapped[2], parts[3])], axis=0
        ).astype(BF16)
        for one in (0, 1):
            def go():
                j = (2 * g + core) * nj + 2 * y + one
                remote(
                    kvs.at[g, one], kvr.at[core, y, g, one], kva_send.at[g], kva_recv.at[g], (peer_scalar(j), me_h)
                ).start()

            if g == 1 and one == 1:
                pl.when(jnp.logical_not(keeps_own))(go)

                @pl.when(keeps_own)
                def _():
                    kvr[core, y, 1, 1] = kvs[1, 1]
            else:
                go()

    keeps_own = jnp.logical_and(core == 1, y == ny - 1)

    def kva_each(g, wait):
        def all_of(n):
            block = kvr.at[core, y, g, pl.ds(0, n)]
            wait(remote(kvs.at[g, pl.ds(0, n)], block, kva_send.at[g], kva_recv.at[g], sibling))

        if g == 0:
            all_of(2)
        else:
            pl.when(keeps_own)(lambda: all_of(1))
            pl.when(jnp.logical_not(keeps_own))(lambda: all_of(2))

    def img_ag(d):
        return remote(kvr.at[core, y], kvr.at[core, y], ag_ssem.at[1], ag_rsem.at[1, d - 1], on_ring(y + d))

    def img_ag_arrival(d):
        block = kvr.at[core, wrap_y(y - d)]
        return remote(block, block, ag_ssem.at[1], ag_rsem.at[1, d - 1], sibling)

    def img_ag_all():
        block = kvr.at[core, pl.ds(0, ny - 1)]
        return remote(block, block, ag_ssem.at[1], ag_rsem.at[1, 0], sibling)

    def img_fwd(side_core):
        block = kvr.at[side_core]
        return remote(block, block, fwd_send.at[1], fwd_recv.at[1], sibling)

    def prepare():
        n_lane = lax.broadcasted_iota(jnp.int32, (n_seq, img_tok), 1)
        i_sub = lax.broadcasted_iota(jnp.int32, (n_seq, img_tok), 0)
        square_s = lax.broadcasted_iota(jnp.int32, (n_seq, n_seq), 0)
        square_l = lax.broadcasted_iota(jnp.int32, (n_seq, n_seq), 1)

        def column(row):
            return jnp.sum(jnp.where(square_s == square_l, row, 0.0), axis=1, keepdims=True)

        slot_col = column(slot_row[...].astype(F32)).astype(jnp.int32)
        first_r = (first_position(start_r.astype(jnp.int32)) >> log2(n_seq)).astype(F32)
        first_c = column(first_r)
        keep_l = lax.broadcasted_iota(jnp.int32, (1, img_tok), 1)
        row_i = jnp.sum(jnp.where(i_sub == peer_of(n_lane, -1), first_c, 0.0), axis=0, keepdims=True)
        place[:, img_tok:] = row_i.astype(jnp.int32) + (keep_l & (KEEP - 1))
        row_t = jnp.sum(jnp.where(slot_col == (n_lane >> log2(KEEP)), first_c, 0.0), axis=0, keepdims=True)
        place[:, :img_tok] = text_row(row_t.astype(jnp.int32), keep_l)
        n_sub = lax.broadcasted_iota(jnp.int32, (img_tok, n_seq), 0)
        i_lane = lax.broadcasted_iota(jnp.int32, (img_tok, n_seq), 1)
        keep_s = lax.broadcasted_iota(jnp.int32, (img_tok, 1), 0)
        row_t = jnp.sum(jnp.where(slot_row[...] == (n_sub >> log2(KEEP)), first_r, 0.0), axis=1, keepdims=True)
        row_t = text_row(row_t.astype(jnp.int32), keep_s)
        pos[...] = row_t
        hot = one_hot(lax.broadcasted_iota(jnp.int32, (img_tok, local_rows), 1) == row_t)
        for i in range(5, 9):
            copies[i].wait()
        text_partial(dot(hot, text_v[...]))
        keys = core == 0
        angles = (pos[text_rows_of(y), :] * n_seq + me_s).astype(F32) * freq[...]
        trig[0] = jnp.where(keys, jnp.cos(angles), 1.0)
        trig[1] = jnp.where(keys, jnp.sin(angles), 0.0)
        for g in (0, 1):
            n = lax.broadcasted_iota(jnp.int32, (mine_rows, 1), 0)
            n = n + ((2 * g + core) * rc + y * mine_rows)
            angles = (my_start + token_of(n)).astype(F32) * freq[...]
            turn[g, 0] = jnp.cos(angles)
            turn[g, 1] = jnp.sin(angles)

    def text_row(first, n):
        e, m = n >> log2(KEEP), n & (KEEP - 1)
        row = e * per_example + m
        return jnp.where(row >= first, row + KEEP, row)

    pl.semaphore_wait(barrier, n_seq - 1 + ny)

    @pl.loop(0, chunks)
    def _(r):
        attend(r)
        if hops > 1:
            ring_copy(r, 0, 1).start()
            ring_copy(r, 1, 1).start()
        else:
            far_slot_ops(r, lambda way: ring_copy(r, way, 1).start())
        sib_copy(r, 0).start()

    prepare()
    copies[9].wait()

    for hop in range(1, hops):
        @pl.loop(0, chunks)
        def _(r):
            for way in (0, 1):
                ring_arrival(r, way, hop).wait_recv()
                if hop + 1 < hops:
                    ring_copy(r, way, hop + 1).start()
                else:
                    @pl.when(farthest_way(r) == way)
                    def _():
                        ring_copy(r, way, hop + 1).start()
                sib_copy(r, hop if way == 0 else hops + hop).start()

        if hop == 1:
            accumulate(0, first=True)
        else:
            accumulate(hop - 1)
            accumulate(hops + hop - 1)
    text_scatter()
    accumulate(hops - 1)
    accumulate(2 * hops - 1)

    @pl.loop(0, chunks + 1)
    def _(r):
        @pl.when(r < chunks)
        def _():
            far_slot_ops(r, lambda way: ring_arrival(r, way, hops).wait_recv())
            sib_copy(r, hops).start()

        @pl.when(r > 0)
        def _():
            send_chunk(r - 1)

        for g in (0, 1):
            @pl.when(r == 2 * g + 2)
            def _():
                img_partial(g)

    img_scatter(0)
    img_scatter(1)
    text_finish()
    img_finish(0)
    img_finish(1)
    text_forward()
    for r in range(chunks):
        take_chunk(r)
    hot = one_hot(lax.broadcasted_iota(jnp.int32, (local_rows, img_tok), 0) == place[:, img_tok:])
    is_image = jnp.sum(hot.astype(F32), axis=1, keepdims=True)
    for g in (0, 1):
        kva_each(g, lambda c: c.wait_recv())
    for d in range(1, ny):
        img_ag(d).start()
    merged_v[...] = jnp.where(is_image > 0.5, dot(hot, tok[...]), text_v[...].astype(F32)).astype(BF16)
    merged_out = pltpu.make_async_copy(merged_v, merged_hbm, out_sem.at[0])
    merged_out.start()
    text_fwd(1 - core).wait_recv()
    hot_text = one_hot(lax.broadcasted_iota(jnp.int32, (local_rows, img_tok), 0) == place[:, :img_tok])
    kv_acc[...] = dot(hot_text, jnp.concatenate([kvfin[0], kvfin[1]], axis=1))
    for d in range(1, ny):
        img_ag_arrival(d).wait_recv()
    img_fwd(core).start()
    img_fwd(1 - core).wait_recv()
    for r in range(chunks):
        kv_img[r * rc:(r + 1) * rc, :] = unpack(kvr[r % 2, :, r // 2].reshape(nj * PACK, 128))
    kv_v[...] = (kv_acc[...] + dot(hot, kv_img[...])).astype(BF16)
    kv_out = pltpu.make_async_copy(kv_v, kv_hbm, out_sem.at[1])
    kv_out.start()

    for way in (0, 1):
        for hop in range(1, hops + 1):
            n = img_tok if hop < hops else img_tok // 2
            block = att.at[0, pl.ds(0, HEADS), pl.ds(0, n)]
            remote(block, block, ring_send.at[way, hop - 1], ring_recv.at[0, way, hop - 1], sibling).wait_send()
    for slot in range(2 * hops):
        sib_all(slot, core).wait_send()
    for r in range(chunks):
        a2a_all(r).wait_send()
    half_copy().wait_send()
    text_rs_all().wait_send()
    text_ag_all().wait_send()
    text_fwd(core).wait_send()
    for g in (0, 1):
        img_half_copy(g).wait_send()
        img_rs_all(g).wait_send()
        kva_each(g, lambda c: c.wait_send())
    img_ag_all().wait_send()
    img_fwd(core).wait_send()
    merged_out.wait()
    kv_out.wait()


def on_device(
    nx,
    vit_query,
    vit_key,
    vit_value,
    image_proj,
    image_slot,
    image_offset,
    text_embed,
    norm_gain,
    kv_weight,
):
    n_seq, n_head = lax.axis_size("seq"), lax.axis_size("head")
    nz, ny = n_seq // nx, n_head // 2
    img_tok, local_rows = vit_query.shape[0], text_embed.shape[0]
    chunks = min(4, nz)
    hops = ny // 2
    d_model = n_head * FEAT
    rows = 2 * img_tok
    rc = img_tok // chunks
    nj = rc // KEEP
    exponent = np.arange(KV_HD // 2, dtype=np.float32) * np.float32(2.0 / KV_HD)
    freq = jnp.power(jnp.float32(10000.0), -jnp.asarray(exponent))[None, :]
    sizes = (n_seq, nz, nx, ny, chunks, img_tok, local_rows, d_model)
    hbm = pl.BlockSpec(memory_space=pltpu.HBM)
    dma = pltpu.SemaphoreType.DMA
    merged, keys_values = pl.pallas_call(
        functools.partial(kernel, sizes),
        out_shape=(
            jax.ShapeDtypeStruct((local_rows, FEAT), BF16),
            jax.ShapeDtypeStruct((local_rows, KV), BF16),
        ),
        in_specs=[hbm] * 10,
        out_specs=(hbm, hbm),
        scratch_shapes=[
            pltpu.VMEM(vit_query.shape, BF16),
            pltpu.VMEM(vit_query.shape, BF16),
            pltpu.VMEM(vit_query.shape, BF16),
            pltpu.VMEM(image_proj.shape, BF16),
            pltpu.VMEM((local_rows, FEAT), BF16),
            pltpu.VMEM(kv_weight.shape, BF16),
            pltpu.VMEM((1, FEAT), F32),
            pltpu.VMEM((1, n_seq), jnp.int32),
            pltpu.VMEM((1, n_seq), jnp.int32),
            pltpu.VMEM((1, 128), F32),
            pltpu.VMEM(vit_query.shape, BF16),
            pltpu.VMEM((ny, 2 * HEADS, img_tok, VIT_HD), BF16),
            pltpu.VMEM((img_tok, FEAT), F32),
            pltpu.VMEM((PACK * nj, PACK * nj), BF16),
            pltpu.VMEM((PACK * nj, PACK * nj), BF16),
            pltpu.VMEM((chunks, nj, PACK, 128), BF16),
            pltpu.VMEM((chunks, nj, PACK, 128), BF16),
            pltpu.VMEM((img_tok, FEAT), BF16),
            pltpu.VMEM((img_tok, FEAT), BF16),
            pltpu.VMEM((1, rows), jnp.int32),
            pltpu.VMEM((img_tok, 1), jnp.int32),
            pltpu.VMEM((2, img_tok // ny, 128), F32),
            pltpu.VMEM((2, 2, rc // ny, 128), F32),
            pltpu.VMEM((2, img_tok, SIDE), F32),
            pltpu.VMEM((img_tok, SIDE), F32),
            pltpu.VMEM((img_tok, SIDE), BF16),
            pltpu.VMEM((img_tok // ny * (ny - 1), SIDE), BF16),
            pltpu.VMEM((2, img_tok, KV_HD), BF16),
            pltpu.VMEM((2, 2, rc, KV + 128), F32),
            pltpu.VMEM((2, rc, KV + 128), F32),
            pltpu.VMEM((2, ny, 2 * rc // ny, SIDE), BF16),
            pltpu.VMEM((2, ny - 1, 2 * rc // ny, SIDE), BF16),
            pltpu.VMEM((2, 2, PACK, 128), BF16),
            pltpu.VMEM((2, ny, 2, 2, PACK, 128), BF16),
            pltpu.VMEM((img_tok, KV), BF16),
            pltpu.VMEM((local_rows, FEAT), BF16),
            pltpu.VMEM((local_rows, KV), BF16),
            pltpu.VMEM((local_rows, KV), F32),
            dma((10,)),
            dma((2,)),
            dma((2, hops)),
            dma((chunks, 2, hops)),
            dma((2 * hops,)),
            dma((2 * hops,)),
            dma((chunks,)),
            dma((chunks,)),
            dma((chunks,)),
            dma((3,)),
            dma((3,)),
            dma((3,)),
            dma((3,)),
            dma((2,)),
            dma((2, ny - 1)),
            dma((2,)),
            dma((2,)),
            dma((2,)),
            dma((2,)),
        ],
        compiler_params=pltpu.CompilerParams(
            collective_id=0, has_side_effects=True, vmem_limit_bytes=60 * 1024 * 1024
        ),
        cost_estimate=pl.CostEstimate(flops=2 * 10**9, bytes_accessed=10**7, transcendentals=200000),
    )(
        vit_query,
        vit_key,
        vit_value,
        image_proj,
        text_embed.reshape(local_rows, FEAT),
        kv_weight,
        norm_gain[None, :],
        image_slot[None, :],
        image_offset[None, :],
        freq,
    )
    return merged[:, None, :], keys_values[:, None, :]


def solution(mesh):
    placed = (
        P("seq", "head"),
        P("seq", "head"),
        P("seq", "head"),
        P(None, "head"),
        P(),
        P(),
        P(None, "seq", "head"),
        P("head"),
        P("head", None),
    )
    return jax.shard_map(
        functools.partial(on_device, 4 if mesh.shape["seq"] % 16 == 0 else 2),
        mesh=mesh,
        in_specs=placed,
        out_specs=(P(None, "seq", "head"), P(None, "seq", None)),
        check_vma=False,
    )
```

```python
import functools
import math

import jax
import jax.numpy as jnp
import numpy as np
from jax import lax
from jax.experimental import pallas as pl
from jax.experimental.pallas import tpu as pltpu
from jax.sharding import PartitionSpec as P

KV_HD = 256
VIT_HD = 128
HEADS = 3
FEAT = 512
KV = 512
KEEP = 4
PACK = FEAT // 128 * KEEP
SIDE = KV_HD + 128
MESH = pl.DeviceIdType.MESH
F32 = jnp.float32
BF16 = jnp.bfloat16


def log2(n):
    return n.bit_length() - 1


def dot(a, b):
    return jnp.dot(a, b, preferred_element_type=F32)


def one_hot(hits):
    return jnp.where(hits, 1.0, 0.0).astype(BF16)


def kernel(
    sizes,
    q_hbm, k_hbm, v_hbm, w_hbm, text_hbm, kvw_hbm, gain_hbm, slot_hbm, offset_hbm, freq_hbm,
    merged_hbm, kv_hbm,
    q_v, k_v, v_v, w_v, text_v, kvw_v, gain, slot_row, offset_row, freq, qp, att, acc, pack_m, unpack_m,
    send_b, recv_b, src_tok, tok, place, pos, trig, turn, halves, sib_b, rs_send, rs_recv, kvfin,
    img_half, img_sib, img_rs, img_rr, kvs, kvr, kv_img, merged_v, kv_v, kv_acc,
    load_sem, out_sem, ring_send, ring_recv, sib_send, sib_recv, far_recv, a2a_send, a2a_recv,
    half_send, half_recv, rs_ssem, rs_rsem, ag_ssem, ag_rsem, fwd_send, fwd_recv, kva_send, kva_recv,
):
    n_seq, nz, nx, ny, chunks, img_tok, example_len, d_model = sizes
    hops = ny // 2
    rc = img_tok // chunks
    nj = rc // KEEP
    local_rows = example_len
    per_example = example_len // n_seq
    text_rr = img_tok // ny
    half_rows = 2 * rc // 2
    mine_rows = half_rows // ny

    me_s = lax.axis_index("seq")
    me_h = lax.axis_index("head")
    y, core = me_h >> 1, me_h & 1
    me_z, me_x = me_s >> log2(nx), me_s & (nx - 1)

    def wrap_y(v):
        return v & (ny - 1)

    far_first = sorted(range(1, ny), key=lambda d: -min(d, ny - d))

    def on_ring(v):
        return (me_s, wrap_y(v) * 2 + core)

    sibling = (me_s, y * 2 + 1 - core)

    def remote(src, dst, ssem, rsem, to):
        return pltpu.make_async_remote_copy(
            src_ref=src, dst_ref=dst, send_sem=ssem, recv_sem=rsem, device_id=to, device_id_type=MESH
        )

    def peer_of(n, sign):
        j = n >> log2(KEEP)
        m = j >> log2(nx)
        mag = (nz - m) >> 1
        dz = mag * (1 - 2 * (m & 1))
        dx = (nx - 1) - (j & (nx - 1))
        return (((me_z + sign * dz) & (nz - 1)) << log2(nx)) + ((me_x + sign * dx) & (nx - 1))

    loads = [
        (slot_hbm, slot_row), (offset_hbm, offset_row), (q_hbm, q_v), (k_hbm, k_v), (v_hbm, v_v),
        (gain_hbm, gain), (freq_hbm, freq), (text_hbm, text_v), (kvw_hbm, kvw_v), (w_hbm, w_v),
    ]
    copies = [pltpu.make_async_copy(a, b, load_sem.at[i]) for i, (a, b) in enumerate(loads)]
    for c in copies:
        c.start()

    barrier = pltpu.get_barrier_semaphore()

    @pl.loop(0, n_seq - 1)
    def _(j):
        pl.semaphore_signal(
            barrier, inc=1, device_id=(peer_of(j << log2(KEEP), 1), me_h), device_id_type=MESH
        )

    for d in range(1, ny):
        pl.semaphore_signal(barrier, inc=1, device_id=on_ring(y + d), device_id_type=MESH)
    pl.semaphore_signal(barrier, inc=1, device_id=sibling, device_id_type=MESH)

    def first_position(start):
        return start + ((me_s - start) & (n_seq - 1))

    copies[0].wait()
    copies[1].wait()
    start_r = (slot_row[...] * example_len + offset_row[...]).astype(F32)
    lanes = lax.broadcasted_iota(jnp.int32, (1, n_seq), 1)
    my_start = jnp.sum(jnp.where(lanes == me_s, start_r, 0.0), axis=1, keepdims=True).astype(jnp.int32)
    n_q = lax.broadcasted_iota(jnp.int32, (img_tok, img_tok), 0)
    col_q = lax.broadcasted_iota(jnp.int32, (img_tok, img_tok), 1)

    def token_of(n):
        return ((peer_of(n, 1) - my_start) & (n_seq - 1)) + n_seq * (n & (KEEP - 1))

    order = one_hot(col_q == token_of(n_q))
    copies[2].wait()
    qp[...] = dot(order, q_v[...]).astype(BF16)
    copies[3].wait()
    copies[4].wait()

    def attend(r):
        rows = pl.ds(pl.multiple_of(r * rc, rc), rc)
        for h in range(HEADS):
            cols = slice(h * VIT_HD, (h + 1) * VIT_HD)
            scores = lax.dot_general(
                qp[rows, cols], k_v[:, cols], (((1,), (1,)), ((), ())), preferred_element_type=F32
            ) / math.sqrt(VIT_HD)
            weights = jnp.exp(scores)
            attention = (weights / jnp.sum(weights, axis=-1, keepdims=True)).astype(BF16)
            att[y, core * HEADS + h, rows, :] = dot(attention, v_v[:, cols]).astype(BF16)

    def block_of(r, origin, side_core):
        rows = pl.ds(pl.multiple_of(r * rc, rc), rc)
        return att.at[origin, pl.ds(side_core * HEADS, HEADS), rows]

    def ring_copy(r, way, hop):
        origin = wrap_y(y - (hop - 1)) if way == 0 else wrap_y(y + (hop - 1))
        block = block_of(r, origin, core)
        to = on_ring(y + 1) if way == 0 else on_ring(y - 1)
        return remote(block, block, ring_send.at[way, hop - 1], ring_recv.at[r, way, hop - 1], to)

    def ring_arrival(r, way, hop):
        origin = wrap_y(y - hop) if way == 0 else wrap_y(y + hop)
        block = block_of(r, origin, core)
        return remote(block, block, ring_send.at[way, hop - 1], ring_recv.at[r, way, hop - 1], sibling)

    def origin_of(slot):
        return wrap_y(y - slot) if slot <= hops else wrap_y(y + (slot - hops))

    def sib_recv_sem(r, slot):
        return far_recv.at[r] if slot == hops else sib_recv.at[slot]

    def sib_copy(r, slot):
        block = block_of(r, origin_of(slot), core)
        return remote(block, block, sib_send.at[slot], sib_recv_sem(r, slot), sibling)

    def sib_arrival(r, slot):
        block = block_of(r, origin_of(slot), 1 - core)
        return remote(block, block, sib_send.at[slot], sib_recv_sem(r, slot), sibling)

    def sib_all(slot, side_core):
        block = att.at[origin_of(slot), pl.ds(side_core * HEADS, HEADS)]
        return remote(block, block, sib_send.at[slot], sib_recv.at[slot], sibling)

    width = 2 * HEADS * VIT_HD

    def weights_of(o):
        return w_v[pl.ds(pl.multiple_of(o * width, width), width), :]

    def accumulate(slot, first=False):
        sib_all(slot, 1 - core).wait_recv()
        o = origin_of(slot)
        lhs = jnp.concatenate([att[o, i] for i in range(2 * HEADS)], axis=1)
        product = dot(lhs, weights_of(o))
        if first:
            acc[...] = product
        else:
            acc[...] += product

    def farthest_way(r):
        return r % 2

    def far_slot_ops(r, op):
        for way in (0, 1):
            @pl.when(farthest_way(r) == way)
            def _():
                op(way)

    def send_chunk(r):
        sib_arrival(r, hops).wait_recv()
        o = origin_of(hops)
        rows = pl.ds(pl.multiple_of(r * rc, rc), rc)
        lhs = jnp.concatenate([att[o, i, rows, :] for i in range(2 * HEADS)], axis=1)
        total = (acc[rows, :] + dot(lhs, weights_of(o))).astype(BF16)
        src_tok[rows, :] = total
        for g in (0, 1):
            @pl.when(r == 2 * g + 1)
            def _():
                img_partial(g)

        stacked = jnp.concatenate(
            [total[:, f * 128:(f + 1) * 128] for f in range(FEAT // 128)], axis=0
        )
        packed = dot(pack_m[...], stacked).astype(BF16)
        send_b[r] = packed.reshape(nj, PACK, 128)

        @pl.when(r == chunks - 1)
        def _():
            recv_b[chunks - 1, nj - 1] = send_b[chunks - 1, nj - 1]

        @pl.when(r < chunks // 2)
        def _():
            start_sends(r, nj)

    def start_sends(r, count):
        @pl.loop(0, count)
        def _(jj):
            remote(
                send_b.at[r, jj], recv_b.at[r, jj], a2a_send.at[r], a2a_recv.at[r],
                (peer_of((r * nj + jj) << log2(KEEP), 1), me_h),
            ).start()

    def a2a_all(r):
        n = nj - 1 if r == chunks - 1 else nj
        return remote(
            send_b.at[r, pl.ds(0, n)], recv_b.at[r, pl.ds(0, n)], a2a_send.at[r], a2a_recv.at[r], sibling
        )

    def unpack(blocks):
        stacked = dot(unpack_m[...], blocks).astype(BF16)
        return jnp.concatenate([stacked[f * rc:(f + 1) * rc] for f in range(FEAT // 128)], axis=1)

    def take_chunk(r):
        a2a_all(r).wait_recv()
        tok[r * rc:(r + 1) * rc, :] = unpack(recv_b[r].reshape(nj * PACK, 128))

    def kv_sums(rows_in):
        widened = rows_in.astype(F32)
        squares = jnp.sum(widened * widened, axis=1, keepdims=True)
        return dot((widened * gain[...]).astype(BF16), kvw_v[...]), squares

    def two_parts(squares):
        high = squares.astype(BF16).astype(F32)
        return high, squares - high

    def inverse(squares):
        return 1.0 / jnp.sqrt(squares / d_model + 1e-06)

    def half_copy():
        return remote(halves.at[1 - core], sib_b, half_send.at[0], half_recv.at[0], sibling)

    def text_partial(rows_in):
        sums, squares = kv_sums(rows_in)
        for half in (0, 1):
            halves[half, :, :KV_HD] = sums[:, half * KV_HD:(half + 1) * KV_HD]
            halves[half, :, KV_HD:] = jnp.broadcast_to(squares, (img_tok, 128))
        half_copy().start()

    def text_rs(d):
        at = pl.multiple_of(wrap_y(y + d) * text_rr, text_rr)
        return remote(
            rs_send.at[pl.ds(at, text_rr)], rs_recv.at[pl.ds((d - 1) * text_rr, text_rr)],
            rs_ssem.at[0], rs_rsem.at[0], on_ring(y + d),
        )

    def text_rs_all():
        everything = rs_recv.at[pl.ds(0, (ny - 1) * text_rr)]
        return remote(everything, everything, rs_ssem.at[0], rs_rsem.at[0], sibling)

    def text_scatter():
        half_copy().wait_recv()
        chip = halves[core] + sib_b[...]
        high, low = two_parts(chip[:, KV_HD:])
        lane = lax.broadcasted_iota(jnp.int32, (img_tok, 128), 1)
        rs_send[:, :KV_HD] = chip[:, :KV_HD].astype(BF16)
        rs_send[:, KV_HD:] = jnp.where(lane < 64, high, low).astype(BF16)
        for d in far_first:
            text_rs(d).start()

    def text_rows_of(o):
        return pl.ds(pl.multiple_of(o * text_rr, text_rr), text_rr)

    def text_ag(d):
        block = kvfin.at[core, text_rows_of(y)]
        return remote(block, block, ag_ssem.at[0], ag_rsem.at[0, d - 1], on_ring(y + d))

    def text_ag_arrival(d):
        block = kvfin.at[core, text_rows_of(wrap_y(y - d))]
        return remote(block, block, ag_ssem.at[0], ag_rsem.at[0, d - 1], sibling)

    def text_ag_all():
        block = kvfin.at[core, pl.ds(0, (ny - 1) * text_rr)]
        return remote(block, block, ag_ssem.at[0], ag_rsem.at[0, 0], sibling)

    def text_fwd(side_core):
        block = kvfin.at[side_core]
        return remote(block, block, fwd_send.at[0], fwd_recv.at[0], sibling)

    def text_finish():
        text_rs_all().wait_recv()
        total = rs_send[text_rows_of(y), :].astype(F32)
        for d in range(1, ny):
            total += rs_recv[(d - 1) * text_rr:d * text_rr, :].astype(F32)
        squares = total[:, KV_HD:KV_HD + 1] + total[:, KV_HD + 64:KV_HD + 65]
        projected = total[:, :KV_HD] * inverse(squares)
        first, second = projected[:, :128], projected[:, 128:]
        kvfin[core, text_rows_of(y), :128] = (first * trig[0] - second * trig[1]).astype(BF16)
        kvfin[core, text_rows_of(y), 128:] = (second * trig[0] + first * trig[1]).astype(BF16)
        for d in far_first:
            text_ag(d).start()

    def text_forward():
        for d in range(1, ny):
            text_ag_arrival(d).wait_recv()
        text_fwd(core).start()

    def img_half_copy(g):
        return remote(img_half.at[g, 1 - core], img_sib.at[g], half_send.at[1 + g], half_recv.at[1 + g], sibling)

    def img_partial(g):
        sums, squares = kv_sums(src_tok[pl.ds(pl.multiple_of(g * 2 * rc, 2 * rc), 2 * rc), :])
        for half in (0, 1):
            rows = slice(half * half_rows, (half + 1) * half_rows)
            img_half[g, half, :, :KV] = sums[rows]
            img_half[g, half, :, KV:] = jnp.broadcast_to(squares[rows], (half_rows, 128))
        img_half_copy(g).start()

    def img_scatter(g):
        img_half_copy(g).wait_recv()
        chip = img_half[g, core] + img_sib[g]
        sums = chip[:, :KV].reshape(ny, mine_rows, KV)
        high, low = two_parts(chip[:, KV:].reshape(ny, mine_rows, 128))
        img_rs[g, :, :, :KV_HD] = jnp.concatenate([sums[:, :, :KV_HD], sums[:, :, KV_HD:]], axis=1).astype(BF16)
        img_rs[g, :, :, KV_HD:] = jnp.concatenate([high, low], axis=1).astype(BF16)
        for d in far_first:
            remote(
                img_rs.at[g, wrap_y(y + d)], img_rr.at[g, d - 1], rs_ssem.at[1 + g], rs_rsem.at[1 + g],
                on_ring(y + d),
            ).start()

    def img_rs_all(g):
        return remote(img_rr.at[g], img_rr.at[g], rs_ssem.at[1 + g], rs_rsem.at[1 + g], sibling)

    def img_finish(g):
        img_rs_all(g).wait_recv()
        total = img_rs[g, y].astype(F32)
        for d in range(ny - 1):
            total += img_rr[g, d].astype(F32)
        m = mine_rows
        scale = inverse(total[:m, KV_HD:KV_HD + 1] + total[m:, KV_HD:KV_HD + 1])
        keys, values = total[:m, :KV_HD] * scale, total[m:, :KV_HD] * scale
        first, second = keys[:, :128], keys[:, 128:]
        cosine, sine = turn[g, 0], turn[g, 1]
        parts = (
            first * cosine - second * sine, second * cosine + first * sine, values[:, :128], values[:, 128:],
        )
        swapped = [pltpu.roll(part, KEEP, axis=0) for part in parts]
        lower = lax.broadcasted_iota(jnp.int32, (m, 128), 0) < KEEP
        kvs[g, 0] = jnp.concatenate(
            [jnp.where(lower, parts[0], swapped[1]), jnp.where(lower, parts[2], swapped[3])], axis=0
        ).astype(BF16)
        kvs[g, 1] = jnp.concatenate(
            [jnp.where(lower, swapped[0], parts[1]), jnp.where(lower, swapped[2], parts[3])], axis=0
        ).astype(BF16)
        for one in (0, 1):
            def go():
                j = (2 * g + core) * nj + 2 * y + one
                remote(
                    kvs.at[g, one], kvr.at[core, y, g, one], kva_send.at[g], kva_recv.at[g], (peer_of(j << log2(KEEP), 1), me_h)
                ).start()

            if g == 1 and one == 1:
                pl.when(jnp.logical_not(keeps_own))(go)

                @pl.when(keeps_own)
                def _():
                    kvr[core, y, 1, 1] = kvs[1, 1]
            else:
                go()

    keeps_own = jnp.logical_and(core == 1, y == ny - 1)

    def kva_each(g, wait):
        def all_of(n):
            block = kvr.at[core, y, g, pl.ds(0, n)]
            wait(remote(kvs.at[g, pl.ds(0, n)], block, kva_send.at[g], kva_recv.at[g], sibling))

        if g == 0:
            all_of(2)
        else:
            pl.when(keeps_own)(lambda: all_of(1))
            pl.when(jnp.logical_not(keeps_own))(lambda: all_of(2))

    def img_ag(d, g):
        block = kvr.at[core, y, g]
        return remote(block, block, ag_ssem.at[1], ag_rsem.at[1, d - 1], on_ring(y + d))

    def img_ag_arrival(d):
        block = kvr.at[core, wrap_y(y - d)]
        return remote(block, block, ag_ssem.at[1], ag_rsem.at[1, d - 1], sibling)

    def img_ag_all():
        block = kvr.at[core, pl.ds(0, ny - 1)]
        return remote(block, block, ag_ssem.at[1], ag_rsem.at[1, 0], sibling)

    def img_fwd_from(o):
        block = kvr.at[core, o]
        return remote(block, block, fwd_send.at[1], fwd_recv.at[1], sibling)

    def img_fwd(side_core):
        block = kvr.at[side_core]
        return remote(block, block, fwd_send.at[1], fwd_recv.at[1], sibling)

    def prepare():
        side = PACK * nj
        row_p = lax.broadcasted_iota(jnp.int32, (side, side), 0)
        col_p = lax.broadcasted_iota(jnp.int32, (side, side), 1)

        def packed_from(q):
            return ((q >> log2(KEEP)) & (FEAT // 128 - 1)) * rc + (q >> log2(PACK)) * KEEP + (q & (KEEP - 1))

        pack_m[...] = one_hot(col_p == packed_from(row_p))
        unpack_m[...] = one_hot(row_p == packed_from(col_p))

        n_lane = lax.broadcasted_iota(jnp.int32, (n_seq, img_tok), 1)
        i_sub = lax.broadcasted_iota(jnp.int32, (n_seq, img_tok), 0)
        square_s = lax.broadcasted_iota(jnp.int32, (n_seq, n_seq), 0)
        square_l = lax.broadcasted_iota(jnp.int32, (n_seq, n_seq), 1)

        def column(row):
            return jnp.sum(jnp.where(square_s == square_l, row, 0.0), axis=1, keepdims=True)

        slot_col = column(slot_row[...].astype(F32)).astype(jnp.int32)
        first_r = (first_position(start_r.astype(jnp.int32)) >> log2(n_seq)).astype(F32)
        first_c = column(first_r)
        keep_l = lax.broadcasted_iota(jnp.int32, (1, img_tok), 1)
        row_i = jnp.sum(jnp.where(i_sub == peer_of(n_lane, -1), first_c, 0.0), axis=0, keepdims=True)
        place[:, img_tok:] = row_i.astype(jnp.int32) + (keep_l & (KEEP - 1))
        row_t = jnp.sum(jnp.where(slot_col == (n_lane >> log2(KEEP)), first_c, 0.0), axis=0, keepdims=True)
        place[:, :img_tok] = text_row(row_t.astype(jnp.int32), keep_l)
        n_sub = lax.broadcasted_iota(jnp.int32, (img_tok, n_seq), 0)
        i_lane = lax.broadcasted_iota(jnp.int32, (img_tok, n_seq), 1)
        keep_s = lax.broadcasted_iota(jnp.int32, (img_tok, 1), 0)
        row_t = jnp.sum(jnp.where(slot_row[...] == (n_sub >> log2(KEEP)), first_r, 0.0), axis=1, keepdims=True)
        row_t = text_row(row_t.astype(jnp.int32), keep_s)
        pos[...] = row_t
        hot = one_hot(lax.broadcasted_iota(jnp.int32, (img_tok, local_rows), 1) == row_t)
        for i in range(5, 9):
            copies[i].wait()
        text_partial(dot(hot, text_v[...]))
        keys = core == 0
        angles = (pos[text_rows_of(y), :] * n_seq + me_s).astype(F32) * freq[...]
        trig[0] = jnp.where(keys, jnp.cos(angles), 1.0)
        trig[1] = jnp.where(keys, jnp.sin(angles), 0.0)
        for g in (0, 1):
            n = lax.broadcasted_iota(jnp.int32, (mine_rows, 1), 0)
            n = n + ((2 * g + core) * rc + y * mine_rows)
            angles = (my_start + token_of(n)).astype(F32) * freq[...]
            turn[g, 0] = jnp.cos(angles)
            turn[g, 1] = jnp.sin(angles)

    def text_row(first, n):
        e, m = n >> log2(KEEP), n & (KEEP - 1)
        row = e * per_example + m
        return jnp.where(row >= first, row + KEEP, row)

    attend(0)
    pl.semaphore_wait(barrier, n_seq - 1 + ny)

    @pl.loop(0, chunks)
    def _(r):
        @pl.when(r > 0)
        def _():
            attend(r)

        if hops > 1:
            ring_copy(r, 0, 1).start()
            ring_copy(r, 1, 1).start()
        else:
            far_slot_ops(r, lambda way: ring_copy(r, way, 1).start())
        sib_copy(r, 0).start()

    prepare()
    copies[9].wait()

    for hop in range(1, hops):
        @pl.loop(0, chunks)
        def _(r):
            for way in (0, 1):
                ring_arrival(r, way, hop).wait_recv()
                if hop + 1 < hops:
                    ring_copy(r, way, hop + 1).start()
                else:
                    @pl.when(farthest_way(r) == way)
                    def _():
                        ring_copy(r, way, hop + 1).start()
                sib_copy(r, hop if way == 0 else hops + hop).start()

        if hop == 1:
            accumulate(0, first=True)
        else:
            accumulate(hop - 1)
            accumulate(hops + hop - 1)
    text_scatter()
    accumulate(hops - 1)
    accumulate(2 * hops - 1)

    @pl.loop(0, chunks + 1)
    def _(r):
        @pl.when(r < chunks)
        def _():
            far_slot_ops(r, lambda way: ring_arrival(r, way, hops).wait_recv())
            sib_copy(r, hops).start()

        @pl.when(r > 0)
        def _():
            send_chunk(r - 1)

        @pl.when(r == 3)
        def _():
            img_scatter(0)

    img_scatter(1)
    img_finish(0)
    img_finish(1)
    for r in range(chunks // 2, chunks):
        start_sends(r, nj - 1 if r == chunks - 1 else nj)
    text_finish()
    hot = one_hot(lax.broadcasted_iota(jnp.int32, (local_rows, img_tok), 0) == place[:, img_tok:])
    is_image = jnp.sum(hot.astype(F32), axis=1, keepdims=True)
    for r in range(chunks // 2):
        take_chunk(r)
    for g in (0, 1):
        kva_each(g, lambda c: c.wait_recv())
        for d in far_first:
            img_ag(d, g).start()
    for r in range(chunks // 2, chunks):
        take_chunk(r)
    text_forward()
    merged_v[...] = jnp.where(is_image > 0.5, dot(hot, tok[...]), text_v[...].astype(F32)).astype(BF16)
    merged_out = pltpu.make_async_copy(merged_v, merged_hbm, out_sem.at[0])
    merged_out.start()
    text_fwd(1 - core).wait_recv()
    hot_text = one_hot(lax.broadcasted_iota(jnp.int32, (local_rows, img_tok), 0) == place[:, :img_tok])
    kv_acc[...] = dot(hot_text, jnp.concatenate([kvfin[0], kvfin[1]], axis=1))
    img_fwd_from(y).start()
    for d in reversed(far_first):
        img_ag_arrival(d).wait_recv()
        img_fwd_from(wrap_y(y - d)).start()

    def unpack_kv(side_core):
        for g in (0, 1):
            rows = pl.ds(pl.multiple_of((2 * g + side_core) * rc, rc), rc)
            kv_img[rows, :] = unpack(kvr[side_core, :, g].reshape(nj * PACK, 128))

    unpack_kv(core)
    img_fwd(1 - core).wait_recv()
    unpack_kv(1 - core)
    kv_out = []
    for half in (0, 1):
        rows = slice(half * local_rows // 2, (half + 1) * local_rows // 2)
        kv_v[rows, :] = (kv_acc[rows, :] + dot(hot[rows], kv_img[...])).astype(BF16)
        kv_out.append(pltpu.make_async_copy(kv_v.at[rows], kv_hbm.at[rows], out_sem.at[1 + half]))
        kv_out[half].start()

    for way in (0, 1):
        for hop in range(1, hops + 1):
            n = img_tok if hop < hops else img_tok // 2
            block = att.at[0, pl.ds(0, HEADS), pl.ds(0, n)]
            remote(block, block, ring_send.at[way, hop - 1], ring_recv.at[0, way, hop - 1], sibling).wait_send()
    for slot in range(2 * hops):
        sib_all(slot, core).wait_send()
    for r in range(chunks):
        a2a_all(r).wait_send()
    half_copy().wait_send()
    text_rs_all().wait_send()
    text_ag_all().wait_send()
    text_fwd(core).wait_send()
    for g in (0, 1):
        img_half_copy(g).wait_send()
        img_rs_all(g).wait_send()
        kva_each(g, lambda c: c.wait_send())
    img_ag_all().wait_send()
    img_fwd(core).wait_send()
    merged_out.wait()
    kv_out[0].wait()
    kv_out[1].wait()


def on_device(
    nx,
    vit_query,
    vit_key,
    vit_value,
    image_proj,
    image_slot,
    image_offset,
    text_embed,
    norm_gain,
    kv_weight,
):
    n_seq, n_head = lax.axis_size("seq"), lax.axis_size("head")
    nz, ny = n_seq // nx, n_head // 2
    img_tok, local_rows = vit_query.shape[0], text_embed.shape[0]
    chunks = min(4, nz)
    hops = ny // 2
    d_model = n_head * FEAT
    rows = 2 * img_tok
    rc = img_tok // chunks
    nj = rc // KEEP
    exponent = np.arange(KV_HD // 2, dtype=np.float32) * np.float32(2.0 / KV_HD)
    freq = jnp.power(jnp.float32(10000.0), -jnp.asarray(exponent))[None, :]
    sizes = (n_seq, nz, nx, ny, chunks, img_tok, local_rows, d_model)
    hbm = pl.BlockSpec(memory_space=pltpu.HBM)
    dma = pltpu.SemaphoreType.DMA
    merged, keys_values = pl.pallas_call(
        functools.partial(kernel, sizes),
        out_shape=(
            jax.ShapeDtypeStruct((local_rows, FEAT), BF16),
            jax.ShapeDtypeStruct((local_rows, KV), BF16),
        ),
        in_specs=[hbm] * 10,
        out_specs=(hbm, hbm),
        scratch_shapes=[
            pltpu.VMEM(vit_query.shape, BF16),
            pltpu.VMEM(vit_query.shape, BF16),
            pltpu.VMEM(vit_query.shape, BF16),
            pltpu.VMEM(image_proj.shape, BF16),
            pltpu.VMEM((local_rows, FEAT), BF16),
            pltpu.VMEM(kv_weight.shape, BF16),
            pltpu.VMEM((1, FEAT), F32),
            pltpu.VMEM((1, n_seq), jnp.int32),
            pltpu.VMEM((1, n_seq), jnp.int32),
            pltpu.VMEM((1, 128), F32),
            pltpu.VMEM(vit_query.shape, BF16),
            pltpu.VMEM((ny, 2 * HEADS, img_tok, VIT_HD), BF16),
            pltpu.VMEM((img_tok, FEAT), F32),
            pltpu.VMEM((PACK * nj, PACK * nj), BF16),
            pltpu.VMEM((PACK * nj, PACK * nj), BF16),
            pltpu.VMEM((chunks, nj, PACK, 128), BF16),
            pltpu.VMEM((chunks, nj, PACK, 128), BF16),
            pltpu.VMEM((img_tok, FEAT), BF16),
            pltpu.VMEM((img_tok, FEAT), BF16),
            pltpu.VMEM((1, rows), jnp.int32),
            pltpu.VMEM((img_tok, 1), jnp.int32),
            pltpu.VMEM((2, img_tok // ny, 128), F32),
            pltpu.VMEM((2, 2, rc // ny, 128), F32),
            pltpu.VMEM((2, img_tok, SIDE), F32),
            pltpu.VMEM((img_tok, SIDE), F32),
            pltpu.VMEM((img_tok, SIDE), BF16),
            pltpu.VMEM((img_tok // ny * (ny - 1), SIDE), BF16),
            pltpu.VMEM((2, img_tok, KV_HD), BF16),
            pltpu.VMEM((2, 2, rc, KV + 128), F32),
            pltpu.VMEM((2, rc, KV + 128), F32),
            pltpu.VMEM((2, ny, 2 * rc // ny, SIDE), BF16),
            pltpu.VMEM((2, ny - 1, 2 * rc // ny, SIDE), BF16),
            pltpu.VMEM((2, 2, PACK, 128), BF16),
            pltpu.VMEM((2, ny, 2, 2, PACK, 128), BF16),
            pltpu.VMEM((img_tok, KV), BF16),
            pltpu.VMEM((local_rows, FEAT), BF16),
            pltpu.VMEM((local_rows, KV), BF16),
            pltpu.VMEM((local_rows, KV), F32),
            dma((10,)),
            dma((3,)),
            dma((2, hops)),
            dma((chunks, 2, hops)),
            dma((2 * hops,)),
            dma((2 * hops,)),
            dma((chunks,)),
            dma((chunks,)),
            dma((chunks,)),
            dma((3,)),
            dma((3,)),
            dma((3,)),
            dma((3,)),
            dma((2,)),
            dma((2, ny - 1)),
            dma((2,)),
            dma((2,)),
            dma((2,)),
            dma((2,)),
        ],
        compiler_params=pltpu.CompilerParams(
            collective_id=0, has_side_effects=True, vmem_limit_bytes=60 * 1024 * 1024
        ),
        cost_estimate=pl.CostEstimate(flops=2 * 10**9, bytes_accessed=10**7, transcendentals=200000),
    )(
        vit_query,
        vit_key,
        vit_value,
        image_proj,
        text_embed.reshape(local_rows, FEAT),
        kv_weight,
        norm_gain[None, :],
        image_slot[None, :],
        image_offset[None, :],
        freq,
    )
    return merged[:, None, :], keys_values[:, None, :]


def solution(mesh):
    placed = (
        P("seq", "head"),
        P("seq", "head"),
        P("seq", "head"),
        P(None, "head"),
        P(),
        P(),
        P(None, "seq", "head"),
        P("head"),
        P("head", None),
    )
    return jax.shard_map(
        functools.partial(on_device, 4 if mesh.shape["seq"] % 16 == 0 else 2),
        mesh=mesh,
        in_specs=placed,
        out_specs=(P(None, "seq", "head"), P(None, "seq", None)),
        check_vma=False,
    )
```
